32 devices in a mesh: grp: 4 (over x, core), dev: 8 (over z, y).
Axes of the slice: x: 2, y: 2, z: 4, core: 2. Of those that a mesh axis runs over, the one named last changes fastest.
Arguments:
- queries: bfloat16 [65536, 768], P(('grp', 'dev')), may hold values from -18 to 18
- passages: bfloat16 [8192, 768], P('dev'), may hold values from -5 to 5
- positives: int32 [512], P(('grp', 'dev')), may hold values from 0 to 63
- mined_blocks: int32 [512, 9], P(('grp', 'dev')), may hold values from 0 to 63, as said below
- counts: int32 [512], P(('grp', 'dev')), may hold values from 1 to 9, as said below
Outputs:
- losses: float32 [512, 128], P(('grp', 'dev'))
- query_grad: bfloat16 [65536, 768], P(('grp', 'dev'))
- passage_grad: float32 [8192, 768], P('dev')
The draws below stay inside these ranges and needn't reach their ends.
Inputs may be any that keep to these rules, and one draw needn't show every extreme that they name: `mined_blocks`: the first counts[b] entries of row b are distinct and differ from positives[b]; later entries are ignored. Over the live entries and the positives of the 16 query blocks of one device, at most 2 distinct blocks have the same id // 8; in every draw some value of id // 8 has 2 distinct blocks on every device. `counts`: on every device some query block has 9.
All inputs are finite; a program needn't handle non-finite values.
Results may differ from the reference program's by a relative error of at most 0.0038.
Values may be sent and summed in bfloat16 or wider, within the bound.
A program may use at most 128 MiB of HBM per device.

```python
import math
import jax
import jax.numpy as jnp
from jax import lax

D = 768
QROWS = 128
PROWS = 128
MAXL = 9
CAP = 2
QB_DEV = 16
PB_DEV = 8
QBLOCKS = 512
QUERIES = 65536
PBLOCKS = 64
PASSAGES = 8192
N_DEV = 8


def route_plan(key):
    base_key = jax.random.fold_in(key, 101)
    keys = jax.random.split(base_key, 10)
    groups = QBLOCKS // QB_DEV
    pool_size = N_DEV * CAP
    star_owner = jax.random.randint(keys[0], (), 0, N_DEV)
    pool_score = jax.random.randint(keys[1], (groups, N_DEV, PB_DEV), 0, 1 << 20) * PB_DEV + jnp.arange(PB_DEV, dtype=jnp.int32)
    picked = jnp.argsort(pool_score, axis=-1)[..., :CAP].astype(jnp.int32)
    pool = (jnp.arange(N_DEV, dtype=jnp.int32)[None, :, None] * PB_DEV + picked).reshape(groups, pool_size)
    pos_owner = (star_owner + 1 + jax.random.randint(keys[2], (groups, QB_DEV), 0, N_DEV - 1)) % N_DEV
    pos_slot = jax.random.randint(keys[3], (groups, QB_DEV), 0, CAP)
    pos_index = (pos_owner * CAP + pos_slot).astype(jnp.int32)
    positives = jnp.take_along_axis(pool, pos_index, axis=1)
    heavy = jax.random.randint(keys[4], (groups, 1), 0, 8) == 0
    level = jnp.where(heavy, MAXL, jax.random.randint(keys[5], (groups, 1), 1, 3))
    raw_counts = jax.random.randint(keys[6], (groups, QB_DEV), 0, 1 << 16) % level + 1
    full_block = jax.random.randint(keys[7], (groups, 1), 0, QB_DEV)
    is_full = jnp.arange(QB_DEV, dtype=jnp.int32)[None, :] == full_block
    counts = jnp.where(is_full, MAXL, raw_counts).astype(jnp.int32)
    popular = (jax.random.randint(keys[8], (groups, 1, pool_size), 0, 4) == 0).astype(jnp.int32)
    noise = jax.random.randint(keys[9], (groups, QB_DEV, pool_size), 0, 1 << 12)
    position = jnp.arange(pool_size, dtype=jnp.int32)
    score = (noise - popular * (1 << 12)) * pool_size + position
    score = jnp.where(position[None, None, :] == pos_index[..., None], 1 << 28, score)
    forced = is_full[..., None] & (position // CAP == star_owner)[None, None, :]
    score = jnp.where(forced, -(1 << 28), score)
    ranking = jnp.argsort(score, axis=-1)[..., :MAXL].astype(jnp.int32)
    wide_pool = jnp.broadcast_to(pool[:, None, :], (groups, QB_DEV, pool_size))
    mined = jnp.take_along_axis(wide_pool, ranking, axis=2)
    return (positives.reshape(QBLOCKS), mined.reshape(QBLOCKS, MAXL), counts.reshape(QBLOCKS))


def passage_field(key):
    field_key = jax.random.fold_in(key, 202)
    return jnp.clip(jax.random.normal(field_key, (PASSAGES, D), jnp.float32), -5.0, 5.0)


def draw_passages(key, part):
    return passage_field(key).astype(jnp.bfloat16)


def draw_queries(key, part):
    query_key = jax.random.fold_in(key, 303)
    values = jnp.clip(jax.random.normal(query_key, (QUERIES, D), jnp.float32), -5.0, 5.0)
    return values.astype(jnp.bfloat16)


def draw_positives(key, part):
    return route_plan(key)[0]


def draw_mined_blocks(key, part):
    return route_plan(key)[1]


def draw_counts(key, part):
    return route_plan(key)[2]


def setup_inputs(seed: int = 0) -> dict:
    key_of = jax.random.split(jax.random.key(seed), 6)
    return {
        "queries": draw_queries(jax.random.fold_in(key_of[5], 71), 0),
        "passages": draw_passages(jax.random.fold_in(key_of[5], 71), 0),
        "positives": draw_positives(jax.random.fold_in(key_of[5], 71), 0),
        "mined_blocks": draw_mined_blocks(jax.random.fold_in(key_of[5], 71), 0),
        "counts": draw_counts(jax.random.fold_in(key_of[5], 71), 0),
    }


def list_entries(positives, mined_blocks, counts):
    total_blocks = positives.shape[0]
    block_ids = jnp.concatenate([positives[:, None], mined_blocks], axis=1).astype(jnp.int32)
    tail_live = jnp.arange(MAXL, dtype=jnp.int32)[None, :] < counts[:, None]
    is_live = jnp.concatenate([jnp.ones((total_blocks, 1), dtype=jnp.bool_), tail_live], axis=1)
    return (block_ids, is_live)

def reference(queries, passages, positives, mined_blocks, counts):
    factor = 1.0 / math.sqrt(D)
    blocks = passages.reshape(PBLOCKS, PROWS, D)
    query_blocks = queries.reshape(QBLOCKS, QROWS, D)
    block_ids, is_live = list_entries(positives, mined_blocks, counts)
    slot_total = MAXL + 1
    diagonal_mask = (jnp.arange(QROWS)[:, None] == jnp.arange(PROWS)[None, :]).astype(jnp.float32)
    target = jnp.where((jnp.arange(slot_total) == 0)[None, :, None], diagonal_mask[:, None, :], jnp.zeros((), jnp.float32))

    def visit(grad_sum, inputs):
        query_rows, index_row, live_row = inputs
        candidates = blocks[index_row].astype(jnp.float32)
        query_wide = query_rows.astype(jnp.float32)
        scores = jnp.einsum('qd,spd->qsp', query_wide, candidates, precision=lax.Precision.HIGHEST) * factor
        scores = jnp.where(live_row[None, :, None], scores, -jnp.inf)
        largest = lax.optimization_barrier(jnp.max(scores, axis=(1, 2), keepdims=True))
        log_total = largest + jnp.log(lax.optimization_barrier(jnp.sum(jnp.exp(scores - largest), axis=(1, 2), keepdims=True)))
        row_losses = log_total[:, 0, 0] - jnp.diagonal(scores[:, 0, :])
        weights = (jnp.exp(scores - log_total) - target).astype(jnp.bfloat16).astype(jnp.float32)
        query_part = jnp.einsum('qsp,spd->qd', weights, candidates, precision=lax.Precision.HIGHEST)
        passage_part = jnp.einsum('qsp,qd->spd', weights, query_wide, precision=lax.Precision.HIGHEST)
        grad_sum = grad_sum.at[index_row].add(passage_part)
        return (grad_sum, (row_losses, query_part.astype(jnp.bfloat16)))
    start = jnp.zeros((PBLOCKS, PROWS, D), jnp.float32)
    grad_sum, outputs = lax.scan(visit, start, (query_blocks, block_ids, is_live))
    losses, query_grad = outputs
    return (losses, query_grad.reshape(QUERIES, D), grad_sum.reshape(PASSAGES, D))
```

```python
import math

import jax
import jax.numpy as jnp
from jax import lax
from jax.sharding import PartitionSpec as P

QROWS = 128
PROWS = 128
MAXL = 9
CAP = 2


def list_entries(positives, mined_blocks, counts):
    total_blocks = positives.shape[0]
    block_ids = jnp.concatenate([positives[:, None], mined_blocks], axis=1)
    tail_live = jnp.arange(MAXL, dtype=jnp.int32)[None, :] < counts[:, None]
    is_live = jnp.concatenate([jnp.ones((total_blocks, 1), dtype=jnp.bool_), tail_live], axis=1)
    return (block_ids, is_live)


def build_table(block_ids, is_live, shard_blocks, owners):
    flat_ids = block_ids.reshape(-1)
    flat_live = is_live.reshape(-1)
    entry_count = flat_ids.shape[0]
    position = jnp.arange(entry_count, dtype=jnp.int32)
    owner_of = flat_ids // shard_blocks
    local_id = flat_ids % shard_blocks
    matching = (flat_ids[:, None] == flat_ids[None, :]) & flat_live[:, None] & flat_live[None, :]
    earlier = position[None, :] < position[:, None]
    leading = flat_live & jnp.logical_not(jnp.any(matching & earlier, axis=1))
    leader = jnp.min(jnp.where(matching, position[None, :], entry_count), axis=1)
    leader = jnp.where(flat_live, leader, 0)
    same_owner = owner_of[:, None] == owner_of[None, :]
    standing = jnp.sum((leading[None, :] & same_owner & earlier).astype(jnp.int32), axis=1)
    place = standing[leader]
    slot_index = jnp.where(flat_live, owner_of * CAP + place, 0).reshape(block_ids.shape)
    owner_range = jnp.arange(owners, dtype=jnp.int32)
    place_range = jnp.arange(CAP, dtype=jnp.int32)
    chosen = (
        leading[:, None, None]
        & (owner_of[:, None, None] == owner_range[None, :, None])
        & (standing[:, None, None] == place_range[None, None, :])
    )
    request = jnp.sum(chosen.astype(jnp.int32) * local_id[:, None, None], axis=0)
    return (slot_index, request)


def dense_pass(queries, fetched, slot_index, is_live, factor):
    block_total = slot_index.shape[0]
    slots = fetched.shape[0]
    width = queries.shape[1]
    flat = fetched.reshape(slots * PROWS, width)
    slot_range = jnp.arange(slots, dtype=jnp.int32)
    used = jnp.any((slot_index[:, :, None] == slot_range) & is_live[:, :, None], axis=1)
    positive = (slot_index[:, 0, None] == slot_range).astype(jnp.float32)
    scores = jnp.einsum("qd,pd->qp", queries, flat, preferred_element_type=jnp.float32) * factor
    scores = scores.reshape(block_total, QROWS, slots, PROWS)
    scores = jnp.where(used[:, None, :, None], scores, -jnp.inf)
    diagonal = jnp.eye(QROWS, PROWS, dtype=jnp.float32)
    target = positive[:, None, :, None] * diagonal[None, :, None, :]
    largest = jnp.max(scores, axis=(2, 3), keepdims=True)
    log_total = largest + jnp.log(jnp.sum(jnp.exp(scores - largest), axis=(2, 3), keepdims=True))
    hit = jnp.sum(jnp.where(target > 0, scores, 0.0), axis=(2, 3))
    losses = log_total[:, :, 0, 0] - hit
    weights = (jnp.exp(scores - log_total) - target).astype(jnp.bfloat16)
    weights = weights.reshape(block_total * QROWS, slots * PROWS)
    query_grad = jnp.einsum("qp,pd->qd", weights, flat, preferred_element_type=jnp.float32)
    slot_grads = jnp.einsum("qp,qd->pd", weights, queries, preferred_element_type=jnp.float32)
    return slot_grads.astype(jnp.bfloat16), (losses, query_grad.astype(jnp.bfloat16))


def body(queries, passages, positives, mined_blocks, counts):
    owners = lax.axis_size("dev")
    width = queries.shape[1]
    shard_blocks = passages.shape[0] // PROWS
    block_total = positives.shape[0]
    block_ids, is_live = list_entries(positives, mined_blocks, counts)
    slot_index, request = build_table(block_ids, is_live, shard_blocks, owners)
    wanted = lax.all_to_all(request, "dev", split_axis=0, concat_axis=0, tiled=True)
    blocks = passages.reshape(shard_blocks, PROWS, width)
    outgoing = blocks[wanted]
    fetched = lax.all_to_all(outgoing, "dev", split_axis=0, concat_axis=0, tiled=True).reshape(
        owners * CAP, PROWS, width
    )
    factor = 1.0 / math.sqrt(width)
    slot_grads, outputs = dense_pass(queries, fetched, slot_index, is_live, factor)
    losses, query_grad = outputs
    returned = lax.all_to_all(
        slot_grads.reshape(owners, CAP, PROWS, width),
        "dev",
        split_axis=0,
        concat_axis=0,
        tiled=True,
    )
    place = (jnp.arange(shard_blocks, dtype=jnp.int32)[:, None] == wanted.reshape(-1)).astype(jnp.bfloat16)
    shard_grad = jnp.einsum(
        "bs,sd->bd",
        place,
        returned.reshape(owners * CAP, PROWS * width),
        preferred_element_type=jnp.float32,
    )
    passage_grad = lax.psum(shard_grad.reshape(shard_blocks * PROWS, width), "grp")
    return (losses, query_grad.reshape(block_total * QROWS, width), passage_grad)


def solution(mesh):
    return jax.shard_map(
        body,
        mesh=mesh,
        in_specs=(
            P(("grp", "dev"), None),
            P("dev", None),
            P(("grp", "dev")),
            P(("grp", "dev"), None),
            P(("grp", "dev")),
        ),
        out_specs=(P(("grp", "dev"), None), P(("grp", "dev"), None), P("dev", None)),
        check_vma=False,
    )
```

```python
import math

import jax
import jax.numpy as jnp
from jax import lax
from jax.sharding import PartitionSpec as P

QROWS = 128
PROWS = 128
MAXL = 9
CAP = 2


def list_entries(positives, mined_blocks, counts):
    total_blocks = positives.shape[0]
    block_ids = jnp.concatenate([positives[:, None], mined_blocks], axis=1)
    tail_live = jnp.arange(MAXL, dtype=jnp.int32)[None, :] < counts[:, None]
    is_live = jnp.concatenate([jnp.ones((total_blocks, 1), dtype=jnp.bool_), tail_live], axis=1)
    return (block_ids, is_live)


def build_table(block_ids, is_live, shard_blocks, owners):
    flat_ids = block_ids.reshape(-1)
    flat_live = is_live.reshape(-1)
    entry_count = flat_ids.shape[0]
    position = jnp.arange(entry_count, dtype=jnp.int32)
    owner_of = flat_ids // shard_blocks
    local_id = flat_ids % shard_blocks
    matching = (flat_ids[:, None] == flat_ids[None, :]) & flat_live[:, None] & flat_live[None, :]
    earlier = position[None, :] < position[:, None]
    leading = flat_live & jnp.logical_not(jnp.any(matching & earlier, axis=1))
    leader = jnp.min(jnp.where(matching, position[None, :], entry_count), axis=1)
    leader = jnp.where(flat_live, leader, 0)
    same_owner = owner_of[:, None] == owner_of[None, :]
    standing = jnp.sum((leading[None, :] & same_owner & earlier).astype(jnp.int32), axis=1)
    place = standing[leader]
    slot_index = jnp.where(flat_live, owner_of * CAP + place, 0).reshape(block_ids.shape)
    owner_range = jnp.arange(owners, dtype=jnp.int32)
    place_range = jnp.arange(CAP, dtype=jnp.int32)
    chosen = (
        leading[:, None, None]
        & (owner_of[:, None, None] == owner_range[None, :, None])
        & (standing[:, None, None] == place_range[None, None, :])
    )
    request = jnp.sum(chosen.astype(jnp.int32) * local_id[:, None, None], axis=0)
    return (slot_index, request)


def dense_pass(queries, fetched, slot_index, is_live, factor):
    block_total = slot_index.shape[0]
    slots = fetched.shape[0]
    width = queries.shape[1]
    flat = fetched.reshape(slots * PROWS, width)
    slot_range = jnp.arange(slots, dtype=jnp.int32)
    used = jnp.any((slot_index[:, :, None] == slot_range) & is_live[:, :, None], axis=1)
    positive = (slot_index[:, 0, None] == slot_range).astype(jnp.float32)
    scores = jnp.einsum("qd,pd->qp", queries, flat, preferred_element_type=jnp.float32) * factor
    scores = scores.reshape(block_total, QROWS, slots, PROWS)
    scores = jnp.where(used[:, None, :, None], scores, -jnp.inf)
    diagonal = jnp.eye(QROWS, PROWS, dtype=jnp.float32)
    target = positive[:, None, :, None] * diagonal[None, :, None, :]
    largest = jnp.max(scores, axis=(2, 3), keepdims=True)
    log_total = largest + jnp.log(jnp.sum(jnp.exp(scores - largest), axis=(2, 3), keepdims=True))
    hit = jnp.sum(jnp.where(target > 0, scores, 0.0), axis=(2, 3))
    losses = log_total[:, :, 0, 0] - hit
    weights = (jnp.exp(scores - log_total) - target).astype(jnp.bfloat16)
    weights = weights.reshape(block_total * QROWS, slots * PROWS)
    query_grad = jnp.einsum("qp,pd->qd", weights, flat, preferred_element_type=jnp.float32)
    slot_grads = jnp.einsum("qp,qd->pd", weights, queries, preferred_element_type=jnp.float32)
    return slot_grads.astype(jnp.bfloat16), (losses, query_grad.astype(jnp.bfloat16))


def body(queries, passages, positives, mined_blocks, counts):
    owners = lax.axis_size("dev")
    groups = lax.axis_size("grp")
    width = queries.shape[1]
    shard_blocks = passages.shape[0] // PROWS
    block_total = positives.shape[0]
    block_ids, is_live = list_entries(positives, mined_blocks, counts)
    slot_index, request = build_table(block_ids, is_live, shard_blocks, owners)
    requests = lax.all_gather(request, ("grp", "dev"), axis=0, tiled=False)
    asked = lax.dynamic_index_in_dim(requests, lax.axis_index("dev"), axis=1, keepdims=False)
    wanted = lax.dynamic_slice_in_dim(asked, lax.axis_index("grp") * owners, owners, axis=0)
    blocks = passages.reshape(shard_blocks, PROWS, width)
    outgoing = jnp.concatenate(
        [
            lax.dynamic_slice_in_dim(blocks, wanted[source, place], 1, axis=0)
            for source in range(owners)
            for place in range(CAP)
        ],
        axis=0,
    ).reshape(owners, CAP, PROWS, width)
    fetched = lax.all_to_all(outgoing, "dev", split_axis=0, concat_axis=0, tiled=True).reshape(
        owners * CAP, PROWS, width
    )
    factor = 1.0 / math.sqrt(width)
    slot_grads, outputs = dense_pass(queries, fetched, slot_index, is_live, factor)
    losses, query_grad = outputs
    part = PROWS // groups
    sending = slot_grads.reshape(owners, CAP, groups, part, width).transpose(2, 0, 1, 3, 4)
    returned = lax.all_to_all(
        sending.reshape(groups * owners, CAP, part, width),
        ("grp", "dev"),
        split_axis=0,
        concat_axis=0,
        tiled=True,
    )
    place = (jnp.arange(shard_blocks, dtype=jnp.int32)[:, None] == asked.reshape(-1)).astype(jnp.bfloat16)
    share = jnp.einsum(
        "bs,sd->bd",
        place,
        returned.reshape(groups * owners * CAP, part * width),
        preferred_element_type=jnp.float32,
    )
    share = share.astype(jnp.bfloat16).reshape(shard_blocks, part, width)
    gathered = lax.all_gather(share, "grp", axis=0, tiled=False)
    passage_grad = gathered.transpose(1, 0, 2, 3).reshape(shard_blocks * PROWS, width)
    passage_grad = passage_grad.astype(jnp.float32)
    return (losses, query_grad.reshape(block_total * QROWS, width), passage_grad)


def solution(mesh):
    return jax.shard_map(
        body,
        mesh=mesh,
        in_specs=(
            P(("grp", "dev"), None),
            P("dev", None),
            P(("grp", "dev")),
            P(("grp", "dev"), None),
            P(("grp", "dev")),
        ),
        out_specs=(P(("grp", "dev"), None), P(("grp", "dev"), None), P("dev", None)),
        check_vma=False,
    )
```

```python
import math

import jax
import jax.numpy as jnp
from jax import lax
from jax.sharding import PartitionSpec as P

QROWS = 128
PROWS = 128
MAXL = 9
CAP = 2


def list_entries(positives, mined_blocks, counts):
    total_blocks = positives.shape[0]
    block_ids = jnp.concatenate([positives[:, None], mined_blocks], axis=1)
    tail_live = jnp.arange(MAXL, dtype=jnp.int32)[None, :] < counts[:, None]
    is_live = jnp.concatenate([jnp.ones((total_blocks, 1), dtype=jnp.bool_), tail_live], axis=1)
    return (block_ids, is_live)


def build_table(block_ids, is_live, shard_blocks, owners):
    flat_ids = block_ids.reshape(-1)
    flat_live = is_live.reshape(-1)
    entry_count = flat_ids.shape[0]
    position = jnp.arange(entry_count, dtype=jnp.int32)
    owner_of = flat_ids // shard_blocks
    local_id = flat_ids % shard_blocks
    matching = (flat_ids[:, None] == flat_ids[None, :]) & flat_live[:, None] & flat_live[None, :]
    earlier = position[None, :] < position[:, None]
    leading = flat_live & jnp.logical_not(jnp.any(matching & earlier, axis=1))
    leader = jnp.min(jnp.where(matching, position[None, :], entry_count), axis=1)
    leader = jnp.where(flat_live, leader, 0)
    same_owner = owner_of[:, None] == owner_of[None, :]
    standing = jnp.sum((leading[None, :] & same_owner & earlier).astype(jnp.int32), axis=1)
    place = standing[leader]
    slot_index = jnp.where(flat_live, owner_of * CAP + place, 0).reshape(block_ids.shape)
    owner_range = jnp.arange(owners, dtype=jnp.int32)
    place_range = jnp.arange(CAP, dtype=jnp.int32)
    chosen = (
        leading[:, None, None]
        & (owner_of[:, None, None] == owner_range[None, :, None])
        & (standing[:, None, None] == place_range[None, None, :])
    )
    request = jnp.sum(chosen.astype(jnp.int32) * local_id[:, None, None], axis=0)
    return (slot_index, request)


def dense_pass(queries, fetched, slot_index, is_live, factor):
    block_total = slot_index.shape[0]
    slots = fetched.shape[0]
    width = queries.shape[1]
    flat = fetched.reshape(slots * PROWS, width)
    slot_range = jnp.arange(slots, dtype=jnp.int32)
    used = jnp.any((slot_index[:, :, None] == slot_range) & is_live[:, :, None], axis=1)
    positive = (slot_index[:, 0, None] == slot_range).astype(jnp.float32)
    scores = jnp.einsum("qd,pd->qp", queries, flat, preferred_element_type=jnp.float32) * factor
    scores = scores.reshape(block_total, QROWS, slots, PROWS)
    scores = jnp.where(used[:, None, :, None], scores, -jnp.inf)
    diagonal = jnp.eye(QROWS, PROWS, dtype=jnp.float32)
    target = positive[:, None, :, None] * diagonal[None, :, None, :]
    largest = jnp.max(scores, axis=(2, 3), keepdims=True)
    log_total = largest + jnp.log(jnp.sum(jnp.exp(scores - largest), axis=(2, 3), keepdims=True))
    hit = jnp.sum(jnp.where(target > 0, scores, 0.0), axis=(2, 3))
    losses = log_total[:, :, 0, 0] - hit
    weights = (jnp.exp(scores - log_total) - target).astype(jnp.bfloat16)
    weights = weights.reshape(block_total * QROWS, slots * PROWS)
    query_grad = jnp.einsum("qp,pd->qd", weights, flat, preferred_element_type=jnp.float32)
    slot_grads = jnp.einsum("qp,qd->pd", weights, queries, preferred_element_type=jnp.float32)
    return slot_grads.astype(jnp.bfloat16), (losses, query_grad.astype(jnp.bfloat16))


def body(queries, passages, positives, mined_blocks, counts):
    owners = lax.axis_size("dev")
    groups = lax.axis_size("grp")
    width = queries.shape[1]
    shard_blocks = passages.shape[0] // PROWS
    block_total = positives.shape[0]
    block_ids, is_live = list_entries(positives, mined_blocks, counts)
    slot_index, request = build_table(block_ids, is_live, shard_blocks, owners)
    wanted = lax.all_to_all(request, "dev", split_axis=0, concat_axis=0, tiled=True)
    asked = lax.all_gather(wanted, "grp", axis=0, tiled=False)
    blocks = passages.reshape(shard_blocks, PROWS, width)
    picks = wanted.reshape(-1)[:, None, None]
    outgoing = jnp.broadcast_to(blocks[0][None], (owners * CAP, PROWS, width))
    for local in range(1, shard_blocks):
        outgoing = jnp.where(picks == local, blocks[local][None], outgoing)
    outgoing = outgoing.reshape(owners, CAP, PROWS, width)
    fetched = lax.all_to_all(outgoing, "dev", split_axis=0, concat_axis=0, tiled=True).reshape(
        owners * CAP, PROWS, width
    )
    factor = 1.0 / math.sqrt(width)
    slot_grads, outputs = dense_pass(queries, fetched, slot_index, is_live, factor)
    losses, query_grad = outputs
    part = PROWS // groups
    sending = slot_grads.reshape(owners, CAP, groups, part, width).transpose(2, 0, 1, 3, 4)
    returned = lax.all_to_all(
        sending.reshape(groups * owners, CAP, part, width),
        ("grp", "dev"),
        split_axis=0,
        concat_axis=0,
        tiled=True,
    )
    place = (jnp.arange(shard_blocks, dtype=jnp.int32)[:, None] == asked.reshape(-1)).astype(jnp.bfloat16)
    share = jnp.einsum(
        "bs,sd->bd",
        place,
        returned.reshape(groups * owners * CAP, part * width),
        preferred_element_type=jnp.float32,
    )
    share = share.astype(jnp.bfloat16).reshape(shard_blocks, part, width)
    gathered = lax.all_gather(share, "grp", axis=0, tiled=False)
    passage_grad = gathered.transpose(1, 0, 2, 3).reshape(shard_blocks * PROWS, width)
    passage_grad = passage_grad.astype(jnp.float32)
    return (losses, query_grad.reshape(block_total * QROWS, width), passage_grad)


def solution(mesh):
    return jax.shard_map(
        body,
        mesh=mesh,
        in_specs=(
            P(("grp", "dev"), None),
            P("dev", None),
            P(("grp", "dev")),
            P(("grp", "dev"), None),
            P(("grp", "dev")),
        ),
        out_specs=(P(("grp", "dev"), None), P(("grp", "dev"), None), P("dev", None)),
        check_vma=False,
    )
```

```python
import functools
import math

import jax
import jax.numpy as jnp
from jax import lax
from jax.experimental import pallas as pl
from jax.experimental.pallas import tpu as pltpu
from jax.sharding import PartitionSpec as P

QROWS = 128
PROWS = 128
MAXL = 9
CAP = 2


def list_entries(positives, mined_blocks, counts):
    total_blocks = positives.shape[0]
    block_ids = jnp.concatenate([positives[:, None], mined_blocks], axis=1)
    tail_live = jnp.arange(MAXL, dtype=jnp.int32)[None, :] < counts[:, None]
    is_live = jnp.concatenate([jnp.ones((total_blocks, 1), dtype=jnp.bool_), tail_live], axis=1)
    return (block_ids, is_live)


def build_table(block_ids, is_live, shard_blocks, owners):
    flat_ids = block_ids.reshape(-1)
    flat_live = is_live.reshape(-1)
    entry_count = flat_ids.shape[0]
    position = jnp.arange(entry_count, dtype=jnp.int32)
    owner_of = flat_ids // shard_blocks
    local_id = flat_ids % shard_blocks
    matching = (flat_ids[:, None] == flat_ids[None, :]) & flat_live[:, None] & flat_live[None, :]
    earlier = position[None, :] < position[:, None]
    leading = flat_live & jnp.logical_not(jnp.any(matching & earlier, axis=1))
    leader = jnp.min(jnp.where(matching, position[None, :], entry_count), axis=1)
    leader = jnp.where(flat_live, leader, 0)
    same_owner = owner_of[:, None] == owner_of[None, :]
    standing = jnp.sum((leading[None, :] & same_owner & earlier).astype(jnp.int32), axis=1)
    place = standing[leader]
    slot_index = jnp.where(flat_live, owner_of * CAP + place, 0).reshape(block_ids.shape)
    owner_range = jnp.arange(owners, dtype=jnp.int32)
    place_range = jnp.arange(CAP, dtype=jnp.int32)
    chosen = (
        leading[:, None, None]
        & (owner_of[:, None, None] == owner_range[None, :, None])
        & (standing[:, None, None] == place_range[None, None, :])
    )
    request = jnp.sum(chosen.astype(jnp.int32) * local_id[:, None, None], axis=0)
    return (slot_index, request)


def pick_kernel(wanted, block_ref, out_ref):
    out_ref[...] = block_ref[...]


def pick_blocks(blocks, wanted):
    _, rows, width = blocks.shape
    return pl.pallas_call(
        pick_kernel,
        grid_spec=pltpu.PrefetchScalarGridSpec(
            num_scalar_prefetch=1,
            grid=(wanted.shape[0],),
            in_specs=[pl.BlockSpec((1, rows, width), lambda i, wanted: (wanted[i], 0, 0))],
            out_specs=pl.BlockSpec((1, rows, width), lambda i, wanted: (i, 0, 0)),
        ),
        out_shape=jax.ShapeDtypeStruct((wanted.shape[0], rows, width), blocks.dtype),
        name="pick",
    )(wanted, blocks)


def sum_kernel(places, piece_ref, out_ref, total):
    total[...] = jnp.zeros_like(total)

    def add(i, carry):
        total[places[i]] += piece_ref[i].astype(jnp.float32)
        return carry

    lax.fori_loop(0, piece_ref.shape[0], add, 0)
    out_ref[...] = total[...].astype(out_ref.dtype)


def sum_pieces(pieces, places, shard_blocks):
    count, part, width = pieces.shape
    return pl.pallas_call(
        sum_kernel,
        grid_spec=pltpu.PrefetchScalarGridSpec(
            num_scalar_prefetch=1,
            grid=(1,),
            in_specs=[pl.BlockSpec((count, part, width), lambda i, places: (0, 0, 0))],
            out_specs=pl.BlockSpec((shard_blocks, part, width), lambda i, places: (0, 0, 0)),
            scratch_shapes=[pltpu.VMEM((shard_blocks, part, width), jnp.float32)],
        ),
        out_shape=jax.ShapeDtypeStruct((shard_blocks, part, width), jnp.bfloat16),
        compiler_params=pltpu.CompilerParams(vmem_limit_bytes=32 * 1024 * 1024),
        name="sum_pieces",
    )(places, pieces)


def weight_kernel(per_tile, factor, positive_slot, query_ref, flat_ref, bias_ref, weight_ref, loss_ref, score_ref):
    tile = pl.program_id(0)
    score_ref[...] = lax.dot_general(
        query_ref[...], flat_ref[...], (((1,), (1,)), ((), ())), preferred_element_type=jnp.float32
    )
    eye = lax.broadcasted_iota(jnp.int32, (QROWS, PROWS), 0) == lax.broadcasted_iota(
        jnp.int32, (QROWS, PROWS), 1
    )
    for block in range(per_tile):
        rows = slice(block * QROWS, (block + 1) * QROWS)
        scores = score_ref[rows, :] * factor + bias_ref[block]
        largest = jnp.max(scores, axis=1, keepdims=True)
        powers = jnp.exp(scores - largest)
        total = jnp.sum(powers, axis=1, keepdims=True)
        inverse = 1.0 / total
        log_total = largest + jnp.log(total)
        weight_ref[rows, :] = (powers * inverse).astype(jnp.bfloat16)
        start = pl.multiple_of(positive_slot[tile * per_tile + block] * PROWS, PROWS)
        own = score_ref[rows, pl.ds(start, PROWS)] * factor
        own_weight = jnp.exp(own - largest) * inverse - eye.astype(jnp.float32)
        weight_ref[rows, pl.ds(start, PROWS)] = own_weight.astype(jnp.bfloat16)
        loss_ref[block] = jnp.sum(jnp.where(eye, log_total - own, 0.0), axis=0, keepdims=True)


def dense_pass(queries, fetched, slot_index, is_live, factor):
    block_total = slot_index.shape[0]
    slots = fetched.shape[0]
    width = queries.shape[1]
    columns = slots * PROWS
    flat = fetched.reshape(columns, width)
    slot_range = jnp.arange(slots, dtype=jnp.int32)
    used = jnp.any((slot_index[:, :, None] == slot_range) & is_live[:, :, None], axis=1)
    bias = jnp.where(used, 0.0, -jnp.inf).astype(jnp.float32)
    bias = jnp.broadcast_to(bias[:, None, :, None], (block_total, 1, slots, PROWS))
    bias = bias.reshape(block_total, 1, columns)
    per_tile = math.gcd(block_total, 4)
    weights, losses = pl.pallas_call(
        functools.partial(weight_kernel, per_tile, factor),
        grid_spec=pltpu.PrefetchScalarGridSpec(
            num_scalar_prefetch=1,
            grid=(block_total // per_tile,),
            in_specs=[
                pl.BlockSpec((per_tile * QROWS, width), lambda i, slot: (i, 0)),
                pl.BlockSpec((columns, width), lambda i, slot: (0, 0)),
                pl.BlockSpec((per_tile, 1, columns), lambda i, slot: (i, 0, 0)),
            ],
            out_specs=[
                pl.BlockSpec((per_tile * QROWS, columns), lambda i, slot: (i, 0)),
                pl.BlockSpec((per_tile, 1, QROWS), lambda i, slot: (i, 0, 0)),
            ],
            scratch_shapes=[pltpu.VMEM((per_tile * QROWS, columns), jnp.float32)],
        ),
        out_shape=[
            jax.ShapeDtypeStruct((block_total * QROWS, columns), jnp.bfloat16),
            jax.ShapeDtypeStruct((block_total, 1, QROWS), jnp.float32),
        ],
        compiler_params=pltpu.CompilerParams(vmem_limit_bytes=52 * 1024 * 1024),
        name="weights",
    )(slot_index[:, 0], queries, flat, bias)
    slot_grads = jnp.einsum("qp,qd->pd", weights, queries, preferred_element_type=jnp.float32)
    slot_grads, weights = lax.optimization_barrier((slot_grads.astype(jnp.bfloat16), weights))
    query_grad = jnp.einsum("qp,pd->qd", weights, flat, preferred_element_type=jnp.float32)
    return slot_grads, (losses.reshape(block_total, QROWS), query_grad.astype(jnp.bfloat16))


def body(queries, passages, positives, mined_blocks, counts):
    owners = lax.axis_size("dev")
    groups = lax.axis_size("grp")
    width = queries.shape[1]
    shard_blocks = passages.shape[0] // PROWS
    block_total = positives.shape[0]
    block_ids, is_live = list_entries(positives, mined_blocks, counts)
    slot_index, request = build_table(block_ids, is_live, shard_blocks, owners)
    wanted = lax.all_to_all(request, "dev", split_axis=0, concat_axis=0, tiled=True)
    asked = lax.all_gather(wanted, "grp", axis=0, tiled=False)
    blocks = passages.reshape(shard_blocks, PROWS, width)
    outgoing = pick_blocks(blocks, wanted.reshape(-1))
    outgoing = outgoing.reshape(owners, CAP, PROWS, width)
    fetched = lax.all_to_all(outgoing, "dev", split_axis=0, concat_axis=0, tiled=True).reshape(
        owners * CAP, PROWS, width
    )
    factor = 1.0 / math.sqrt(width)
    slot_grads, outputs = dense_pass(queries, fetched, slot_index, is_live, factor)
    losses, query_grad = outputs
    part = PROWS // groups
    sending = slot_grads.reshape(owners, CAP, groups, part, width).transpose(2, 0, 1, 3, 4)
    returned = lax.all_to_all(
        sending.reshape(groups * owners, CAP, part, width),
        ("grp", "dev"),
        split_axis=0,
        concat_axis=0,
        tiled=True,
    )
    pieces = returned.reshape(groups * owners * CAP, part, width)
    share = sum_pieces(pieces, asked.reshape(-1), shard_blocks)
    gathered = lax.all_gather(share, "grp", axis=0, tiled=False)
    passage_grad = gathered.transpose(1, 0, 2, 3).reshape(shard_blocks * PROWS, width)
    passage_grad = passage_grad.astype(jnp.float32)
    return (losses, query_grad.reshape(block_total * QROWS, width), passage_grad)


def solution(mesh):
    return jax.shard_map(
        body,
        mesh=mesh,
        in_specs=(
            P(("grp", "dev"), None),
            P("dev", None),
            P(("grp", "dev")),
            P(("grp", "dev"), None),
            P(("grp", "dev")),
        ),
        out_specs=(P(("grp", "dev"), None), P(("grp", "dev"), None), P("dev", None)),
        check_vma=False,
    )
```

```python
import functools
import math

import jax
import jax.numpy as jnp
from jax import lax
from jax.experimental import pallas as pl
from jax.experimental.pallas import tpu as pltpu
from jax.sharding import PartitionSpec as P

QROWS = 128
PROWS = 128
MAXL = 9
CAP = 2


def list_entries(positives, mined_blocks, counts):
    total_blocks = positives.shape[0]
    block_ids = jnp.concatenate([positives[:, None], mined_blocks], axis=1)
    tail_live = jnp.arange(MAXL, dtype=jnp.int32)[None, :] < counts[:, None]
    is_live = jnp.concatenate([jnp.ones((total_blocks, 1), dtype=jnp.bool_), tail_live], axis=1)
    return (block_ids, is_live)


def build_table(block_ids, is_live, shard_blocks, owners):
    flat_ids = block_ids.reshape(-1)
    flat_live = is_live.reshape(-1)
    entry_count = flat_ids.shape[0]
    position = jnp.arange(entry_count, dtype=jnp.int32)
    owner_of = flat_ids // shard_blocks
    local_id = flat_ids % shard_blocks
    matching = (flat_ids[:, None] == flat_ids[None, :]) & flat_live[:, None] & flat_live[None, :]
    earlier = position[None, :] < position[:, None]
    leading = flat_live & jnp.logical_not(jnp.any(matching & earlier, axis=1))
    leader = jnp.min(jnp.where(matching, position[None, :], entry_count), axis=1)
    leader = jnp.where(flat_live, leader, 0)
    same_owner = owner_of[:, None] == owner_of[None, :]
    standing = jnp.sum((leading[None, :] & same_owner & earlier).astype(jnp.int32), axis=1)
    place = standing[leader]
    slot_index = jnp.where(flat_live, owner_of * CAP + place, 0).reshape(block_ids.shape)
    owner_range = jnp.arange(owners, dtype=jnp.int32)
    place_range = jnp.arange(CAP, dtype=jnp.int32)
    chosen = (
        leading[:, None, None]
        & (owner_of[:, None, None] == owner_range[None, :, None])
        & (standing[:, None, None] == place_range[None, None, :])
    )
    request = jnp.sum(chosen.astype(jnp.int32) * local_id[:, None, None], axis=0)
    return (slot_index, request)


def pick_kernel(per_step, wanted, block_ref, out_ref):
    step = pl.program_id(0)
    for place in range(per_step):
        out_ref[place] = block_ref[wanted[step * per_step + place]]


def pick_blocks(blocks, wanted):
    held, rows, width = blocks.shape
    count = wanted.shape[0]
    per_step = math.gcd(count, 4)
    return pl.pallas_call(
        functools.partial(pick_kernel, per_step),
        grid_spec=pltpu.PrefetchScalarGridSpec(
            num_scalar_prefetch=1,
            grid=(count // per_step,),
            in_specs=[pl.BlockSpec((held, rows, width), lambda i, wanted: (0, 0, 0))],
            out_specs=pl.BlockSpec((per_step, rows, width), lambda i, wanted: (i, 0, 0)),
        ),
        out_shape=jax.ShapeDtypeStruct((count, rows, width), blocks.dtype),
        compiler_params=pltpu.CompilerParams(vmem_limit_bytes=16 * 1024 * 1024),
        name="pick",
    )(wanted, blocks)


def sum_kernel(places, piece_ref, out_ref, total):
    total[...] = jnp.zeros_like(total)

    def add(i, carry):
        total[places[i]] += piece_ref[i].astype(jnp.float32)
        return carry

    lax.fori_loop(0, piece_ref.shape[0], add, 0)
    out_ref[...] = total[...].astype(out_ref.dtype)


def sum_pieces(pieces, places, shard_blocks):
    count, part, width = pieces.shape
    return pl.pallas_call(
        sum_kernel,
        grid_spec=pltpu.PrefetchScalarGridSpec(
            num_scalar_prefetch=1,
            grid=(1,),
            in_specs=[pl.BlockSpec((count, part, width), lambda i, places: (0, 0, 0))],
            out_specs=pl.BlockSpec((shard_blocks, part, width), lambda i, places: (0, 0, 0)),
            scratch_shapes=[pltpu.VMEM((shard_blocks, part, width), jnp.float32)],
        ),
        out_shape=jax.ShapeDtypeStruct((shard_blocks, part, width), jnp.bfloat16),
        compiler_params=pltpu.CompilerParams(vmem_limit_bytes=32 * 1024 * 1024),
        name="sum_pieces",
    )(places, pieces)


def weight_kernel(per_tile, factor, positive_slot, query_ref, flat_ref, bias_ref, weight_ref, loss_ref, score_ref):
    tile = pl.program_id(0)
    score_ref[...] = lax.dot_general(
        query_ref[...], flat_ref[...], (((1,), (1,)), ((), ())), preferred_element_type=jnp.float32
    )
    eye = lax.broadcasted_iota(jnp.int32, (QROWS, PROWS), 0) == lax.broadcasted_iota(
        jnp.int32, (QROWS, PROWS), 1
    )
    for block in range(per_tile):
        rows = slice(block * QROWS, (block + 1) * QROWS)
        scores = score_ref[rows, :] * factor + bias_ref[block]
        largest = jnp.max(scores, axis=1, keepdims=True)
        powers = jnp.exp(scores - largest)
        total = jnp.sum(powers, axis=1, keepdims=True)
        inverse = 1.0 / total
        log_total = largest + jnp.log(total)
        weight_ref[rows, :] = (powers * inverse).astype(jnp.bfloat16)
        start = pl.multiple_of(positive_slot[tile * per_tile + block] * PROWS, PROWS)
        own = score_ref[rows, pl.ds(start, PROWS)] * factor
        own_weight = jnp.exp(own - largest) * inverse - eye.astype(jnp.float32)
        weight_ref[rows, pl.ds(start, PROWS)] = own_weight.astype(jnp.bfloat16)
        loss_ref[block] = jnp.sum(jnp.where(eye, log_total - own, 0.0), axis=0, keepdims=True)


def dense_pass(queries, fetched, slot_index, is_live, factor):
    block_total = slot_index.shape[0]
    slots = fetched.shape[0]
    width = queries.shape[1]
    columns = slots * PROWS
    flat = fetched.reshape(columns, width)
    slot_range = jnp.arange(slots, dtype=jnp.int32)
    used = jnp.any((slot_index[:, :, None] == slot_range) & is_live[:, :, None], axis=1)
    bias = jnp.where(used, 0.0, -jnp.inf).astype(jnp.float32)
    bias = jnp.broadcast_to(bias[:, None, :, None], (block_total, 1, slots, PROWS))
    bias = bias.reshape(block_total, 1, columns)
    per_tile = math.gcd(block_total, 4)
    weights, losses = pl.pallas_call(
        functools.partial(weight_kernel, per_tile, factor),
        grid_spec=pltpu.PrefetchScalarGridSpec(
            num_scalar_prefetch=1,
            grid=(block_total // per_tile,),
            in_specs=[
                pl.BlockSpec((per_tile * QROWS, width), lambda i, slot: (i, 0)),
                pl.BlockSpec((columns, width), lambda i, slot: (0, 0)),
                pl.BlockSpec((per_tile, 1, columns), lambda i, slot: (i, 0, 0)),
            ],
            out_specs=[
                pl.BlockSpec((per_tile * QROWS, columns), lambda i, slot: (i, 0)),
                pl.BlockSpec((per_tile, 1, QROWS), lambda i, slot: (i, 0, 0)),
            ],
            scratch_shapes=[pltpu.VMEM((per_tile * QROWS, columns), jnp.float32)],
        ),
        out_shape=[
            jax.ShapeDtypeStruct((block_total * QROWS, columns), jnp.bfloat16),
            jax.ShapeDtypeStruct((block_total, 1, QROWS), jnp.float32),
        ],
        compiler_params=pltpu.CompilerParams(vmem_limit_bytes=52 * 1024 * 1024),
        name="weights",
    )(slot_index[:, 0], queries, flat, bias)
    slot_grads = jnp.einsum("qp,qd->pd", weights, queries, preferred_element_type=jnp.float32)
    slot_grads, weights = lax.optimization_barrier((slot_grads.astype(jnp.bfloat16), weights))
    query_grad = jnp.einsum("qp,pd->qd", weights, flat, preferred_element_type=jnp.float32)
    return slot_grads, (losses.reshape(block_total, QROWS), query_grad.astype(jnp.bfloat16))


def body(queries, passages, positives, mined_blocks, counts):
    owners = lax.axis_size("dev")
    groups = lax.axis_size("grp")
    width = queries.shape[1]
    shard_blocks = passages.shape[0] // PROWS
    block_total = positives.shape[0]
    block_ids, is_live = list_entries(positives, mined_blocks, counts)
    slot_index, request = build_table(block_ids, is_live, shard_blocks, owners)
    wanted = lax.all_to_all(request, "dev", split_axis=0, concat_axis=0, tiled=True)
    asked = lax.all_gather(wanted, "grp", axis=0, tiled=False)
    blocks = passages.reshape(shard_blocks, PROWS, width)
    outgoing = pick_blocks(blocks, wanted.reshape(-1))
    outgoing = outgoing.reshape(owners, CAP, PROWS, width)
    fetched = lax.all_to_all(outgoing, "dev", split_axis=0, concat_axis=0, tiled=True).reshape(
        owners * CAP, PROWS, width
    )
    factor = 1.0 / math.sqrt(width)
    slot_grads, outputs = dense_pass(queries, fetched, slot_index, is_live, factor)
    losses, query_grad = outputs
    part = PROWS // groups
    sending = slot_grads.reshape(owners, CAP, groups, part, width).transpose(2, 0, 1, 3, 4)
    returned = lax.all_to_all(
        sending.reshape(groups * owners, CAP, part, width),
        ("grp", "dev"),
        split_axis=0,
        concat_axis=0,
        tiled=True,
    )
    pieces = returned.reshape(groups * owners * CAP, part, width)
    share = sum_pieces(pieces, asked.reshape(-1), shard_blocks)
    gathered = lax.all_gather(share, "grp", axis=0, tiled=False)
    passage_grad = gathered.transpose(1, 0, 2, 3).reshape(shard_blocks * PROWS, width)
    passage_grad = passage_grad.astype(jnp.float32)
    return (losses, query_grad.reshape(block_total * QROWS, width), passage_grad)


def solution(mesh):
    return jax.shard_map(
        body,
        mesh=mesh,
        in_specs=(
            P(("grp", "dev"), None),
            P("dev", None),
            P(("grp", "dev")),
            P(("grp", "dev"), None),
            P(("grp", "dev")),
        ),
        out_specs=(P(("grp", "dev"), None), P(("grp", "dev"), None), P("dev", None)),
        check_vma=False,
    )
```

```python
import functools
import math

import jax
import jax.numpy as jnp
from jax import lax
from jax.experimental import pallas as pl
from jax.experimental.pallas import tpu as pltpu
from jax.sharding import PartitionSpec as P

QROWS = 128
PROWS = 128
MAXL = 9
CAP = 2


def list_entries(positives, mined_blocks, counts):
    total_blocks = positives.shape[0]
    block_ids = jnp.concatenate([positives[:, None], mined_blocks], axis=1)
    tail_live = jnp.arange(MAXL, dtype=jnp.int32)[None, :] < counts[:, None]
    is_live = jnp.concatenate([jnp.ones((total_blocks, 1), dtype=jnp.bool_), tail_live], axis=1)
    return (block_ids, is_live)


def build_table(block_ids, is_live, shard_blocks, owners):
    flat_ids = block_ids.reshape(-1)
    flat_live = is_live.reshape(-1)
    entry_count = flat_ids.shape[0]
    position = jnp.arange(entry_count, dtype=jnp.int32)
    owner_of = flat_ids // shard_blocks
    local_id = flat_ids % shard_blocks
    matching = (flat_ids[:, None] == flat_ids[None, :]) & flat_live[:, None] & flat_live[None, :]
    earlier = position[None, :] < position[:, None]
    leading = flat_live & jnp.logical_not(jnp.any(matching & earlier, axis=1))
    leader = jnp.min(jnp.where(matching, position[None, :], entry_count), axis=1)
    leader = jnp.where(flat_live, leader, 0)
    same_owner = owner_of[:, None] == owner_of[None, :]
    standing = jnp.sum((leading[None, :] & same_owner & earlier).astype(jnp.int32), axis=1)
    place = standing[leader]
    slot_index = jnp.where(flat_live, owner_of * CAP + place, 0).reshape(block_ids.shape)
    owner_range = jnp.arange(owners, dtype=jnp.int32)
    place_range = jnp.arange(CAP, dtype=jnp.int32)
    chosen = (
        leading[:, None, None]
        & (owner_of[:, None, None] == owner_range[None, :, None])
        & (standing[:, None, None] == place_range[None, None, :])
    )
    request = jnp.sum(chosen.astype(jnp.int32) * local_id[:, None, None], axis=0)
    return (slot_index, request)


def pick_kernel(per_step, wanted, block_ref, out_ref):
    step = pl.program_id(0)
    for place in range(per_step):
        out_ref[place] = block_ref[wanted[step * per_step + place]]


def pick_blocks(blocks, wanted):
    held, rows, width = blocks.shape
    count = wanted.shape[0]
    per_step = math.gcd(count, 4)
    return pl.pallas_call(
        functools.partial(pick_kernel, per_step),
        grid_spec=pltpu.PrefetchScalarGridSpec(
            num_scalar_prefetch=1,
            grid=(count // per_step,),
            in_specs=[pl.BlockSpec((held, rows, width), lambda i, wanted: (0, 0, 0))],
            out_specs=pl.BlockSpec((per_step, rows, width), lambda i, wanted: (i, 0, 0)),
        ),
        out_shape=jax.ShapeDtypeStruct((count, rows, width), blocks.dtype),
        compiler_params=pltpu.CompilerParams(vmem_limit_bytes=16 * 1024 * 1024),
        name="pick",
    )(wanted, blocks)


def sum_kernel(places, piece_ref, out_ref, total):
    total[...] = jnp.zeros_like(total)

    def add(i, carry):
        total[places[i]] += piece_ref[i].astype(jnp.float32)
        return carry

    lax.fori_loop(0, piece_ref.shape[0], add, 0)
    out_ref[...] = total[...].astype(out_ref.dtype)


def sum_pieces(pieces, places, shard_blocks):
    count, part, width = pieces.shape
    return pl.pallas_call(
        sum_kernel,
        grid_spec=pltpu.PrefetchScalarGridSpec(
            num_scalar_prefetch=1,
            grid=(1,),
            in_specs=[pl.BlockSpec((count, part, width), lambda i, places: (0, 0, 0))],
            out_specs=pl.BlockSpec((shard_blocks, part, width), lambda i, places: (0, 0, 0)),
            scratch_shapes=[pltpu.VMEM((shard_blocks, part, width), jnp.float32)],
        ),
        out_shape=jax.ShapeDtypeStruct((shard_blocks, part, width), jnp.bfloat16),
        compiler_params=pltpu.CompilerParams(vmem_limit_bytes=32 * 1024 * 1024),
        name="sum_pieces",
    )(places, pieces)


def weight_kernel(per_tile, factor, positive_slot, query_ref, flat_ref, bias_ref, weight_ref, loss_ref, score_ref):
    tile = pl.program_id(0)
    for first in range(0, per_tile, 2):
        pair = slice(first * QROWS, min(first + 2, per_tile) * QROWS)
        score_ref[pair, :] = lax.dot_general(
            query_ref[pair, :], flat_ref[...], (((1,), (1,)), ((), ())), preferred_element_type=jnp.float32
        )
    eye = lax.broadcasted_iota(jnp.int32, (QROWS, PROWS), 0) == lax.broadcasted_iota(
        jnp.int32, (QROWS, PROWS), 1
    )
    for block in range(per_tile):
        rows = slice(block * QROWS, (block + 1) * QROWS)
        scores = score_ref[rows, :] * factor + bias_ref[block]
        largest = jnp.max(scores, axis=1, keepdims=True)
        powers = jnp.exp(scores - largest)
        total = jnp.sum(powers, axis=1, keepdims=True)
        inverse = 1.0 / total
        log_total = largest + jnp.log(total)
        weight_ref[rows, :] = (powers * inverse).astype(jnp.bfloat16)
        start = pl.multiple_of(positive_slot[tile * per_tile + block] * PROWS, PROWS)
        own = score_ref[rows, pl.ds(start, PROWS)] * factor
        own_weight = jnp.exp(own - largest) * inverse - eye.astype(jnp.float32)
        weight_ref[rows, pl.ds(start, PROWS)] = own_weight.astype(jnp.bfloat16)
        loss_ref[block] = jnp.sum(jnp.where(eye, log_total - own, 0.0), axis=0, keepdims=True)


def dense_pass(queries, fetched, slot_index, is_live, factor):
    block_total = slot_index.shape[0]
    slots = fetched.shape[0]
    width = queries.shape[1]
    columns = slots * PROWS
    flat = fetched.reshape(columns, width)
    slot_range = jnp.arange(slots, dtype=jnp.int32)
    used = jnp.any((slot_index[:, :, None] == slot_range) & is_live[:, :, None], axis=1)
    bias = jnp.where(used, 0.0, -jnp.inf).astype(jnp.float32)
    bias = jnp.broadcast_to(bias[:, None, :, None], (block_total, 1, slots, PROWS))
    bias = bias.reshape(block_total, 1, columns)
    per_tile = math.gcd(block_total, 4)
    weights, losses = pl.pallas_call(
        functools.partial(weight_kernel, per_tile, factor),
        grid_spec=pltpu.PrefetchScalarGridSpec(
            num_scalar_prefetch=1,
            grid=(block_total // per_tile,),
            in_specs=[
                pl.BlockSpec((per_tile * QROWS, width), lambda i, slot: (i, 0)),
                pl.BlockSpec((columns, width), lambda i, slot: (0, 0)),
                pl.BlockSpec((per_tile, 1, columns), lambda i, slot: (i, 0, 0)),
            ],
            out_specs=[
                pl.BlockSpec((per_tile * QROWS, columns), lambda i, slot: (i, 0)),
                pl.BlockSpec((per_tile, 1, QROWS), lambda i, slot: (i, 0, 0)),
            ],
            scratch_shapes=[pltpu.VMEM((per_tile * QROWS, columns), jnp.float32)],
        ),
        out_shape=[
            jax.ShapeDtypeStruct((block_total * QROWS, columns), jnp.bfloat16),
            jax.ShapeDtypeStruct((block_total, 1, QROWS), jnp.float32),
        ],
        compiler_params=pltpu.CompilerParams(vmem_limit_bytes=52 * 1024 * 1024),
        name="weights",
    )(slot_index[:, 0], queries, flat, bias)
    slot_grads = jnp.einsum("qp,qd->pd", weights, queries, preferred_element_type=jnp.float32)
    slot_grads, weights = lax.optimization_barrier((slot_grads.astype(jnp.bfloat16), weights))
    query_grad = jnp.einsum("qp,pd->qd", weights, flat, preferred_element_type=jnp.float32)
    return slot_grads, (losses.reshape(block_total, QROWS), query_grad.astype(jnp.bfloat16))


def body(queries, passages, positives, mined_blocks, counts):
    owners = lax.axis_size("dev")
    groups = lax.axis_size("grp")
    width = queries.shape[1]
    shard_blocks = passages.shape[0] // PROWS
    block_total = positives.shape[0]
    block_ids, is_live = list_entries(positives, mined_blocks, counts)
    slot_index, request = build_table(block_ids, is_live, shard_blocks, owners)
    wanted = lax.all_to_all(request, "dev", split_axis=0, concat_axis=0, tiled=True)
    asked = lax.all_gather(wanted, "grp", axis=0, tiled=False)
    blocks = passages.reshape(shard_blocks, PROWS, width)
    outgoing = pick_blocks(blocks, wanted.reshape(-1))
    outgoing = outgoing.reshape(owners, CAP, PROWS, width)
    fetched = lax.all_to_all(outgoing, "dev", split_axis=0, concat_axis=0, tiled=True).reshape(
        owners * CAP, PROWS, width
    )
    factor = 1.0 / math.sqrt(width)
    slot_grads, outputs = dense_pass(queries, fetched, slot_index, is_live, factor)
    losses, query_grad = outputs
    part = PROWS // groups
    sending = slot_grads.reshape(owners, CAP, groups, part, width).transpose(2, 0, 1, 3, 4)
    returned = lax.all_to_all(
        sending.reshape(groups * owners, CAP, part, width),
        ("grp", "dev"),
        split_axis=0,
        concat_axis=0,
        tiled=True,
    )
    pieces = returned.reshape(groups * owners * CAP, part, width)
    share = sum_pieces(pieces, asked.reshape(-1), shard_blocks)
    gathered = lax.all_gather(share, "grp", axis=0, tiled=False)
    passage_grad = gathered.transpose(1, 0, 2, 3).reshape(shard_blocks * PROWS, width)
    passage_grad = passage_grad.astype(jnp.float32)
    return (losses, query_grad.reshape(block_total * QROWS, width), passage_grad)


def solution(mesh):
    return jax.shard_map(
        body,
        mesh=mesh,
        in_specs=(
            P(("grp", "dev"), None),
            P("dev", None),
            P(("grp", "dev")),
            P(("grp", "dev"), None),
            P(("grp", "dev")),
        ),
        out_specs=(P(("grp", "dev"), None), P(("grp", "dev"), None), P("dev", None)),
        check_vma=False,
    )
```
